32 devices in a mesh: groups: 2 (over y), tile: 4 (over z), chan: 2 (over x), sub: 2 (over core).
Axes of the slice: x: 2, y: 2, z: 4, core: 2. Of those that a mesh axis runs over, the one named last changes fastest.
Arguments:
- residual: float32 [8, 8, 64, 128], P(('groups', 'tile'), None, 'sub'), parts along dimension 0, may hold values from -6 to 6
- coefficients: bfloat16 [8, 8, 128, 64, 128], P(('groups', 'tile'), None, 'chan', 'sub'), parts along dimension 0, may hold values from -6 to 6
- filter_store: float32 [16, 128, 2048], P(('groups', 'tile'), 'chan'), parts along dimension 0, may hold values from -6.4 to 6.4
- plan: int32 [2], replicated, may hold values from 0 to 7
- owner: int32 [8], replicated, may hold values from 0 to 7, as said below
Outputs:
- residual_out: float32 [8, 8, 64, 128], P(('groups', 'tile'), None, 'sub'), parts along dimension 0
- new_coefficients: bfloat16 [8, 2, 128, 64, 128], P(('groups', 'tile'), None, 'chan', 'sub'), parts along dimension 0
- store_out: float32 [16, 128, 2048], P(('groups', 'tile'), 'chan'), parts along dimension 0
The draws below stay inside these ranges and needn't reach their ends.
There are 2 independent parts, one for each index of `groups`. The reference program is written for one: setup_inputs(seed, part) draws one part's arguments, and reference() takes and returns one part's arrays. A program takes and returns all parts, laid end to end along the dimension named above; an argument that names none is the same for every part. Nothing has to cross between parts.
Inputs may be any that keep to these rules, and one draw needn't show every extreme that they name: `owner`: distinct slots, one for each of the 8 blocks; slot s lies on tile device s // 2 at position s % 2.
All inputs are finite; a program needn't handle non-finite values.
Results may differ from the reference program's by a relative error of at most 0.017.
Values may be sent and summed in bfloat16 or wider, within the bound.
A program may use at most 128 MiB of HBM per device.

```python
import math
import jax
import jax.numpy as jnp
from jax import lax

C = 8
PATCH = 16
KB = 128
BLOCKS = 8
STEPS = 2
COLS = 128
FEAT = 2048
TILES = 4
HEIGHT = 64
SLOTS_ALL = 8


def draw_filter_store(key, part):
    first, second = jax.random.split(key)
    spread = jnp.exp(jax.random.uniform(first, (SLOTS_ALL, KB, 1), minval=math.log(0.4), maxval=math.log(1.6)))
    values = jnp.clip(jax.random.normal(second, (SLOTS_ALL, KB, FEAT)), -4.0, 4.0)
    return (spread * values).astype(jnp.float32)


def draw_owner(key, part):
    return jax.random.permutation(key, SLOTS_ALL)[:BLOCKS].astype(jnp.int32)


def steps_of(key, extent, cuts, least, largest):
    loudness = 1.0
    for axis_at, parts in cuts:
        steps = jax.random.uniform(jax.random.fold_in(jax.random.fold_in(key, 6), axis_at), (parts,), jnp.float32, least / len(cuts), largest / len(cuts))
        loudness = loudness * jnp.repeat(jnp.exp(steps), extent[axis_at] // parts).reshape((-1,) + (1,) * (len(extent) - 1 - axis_at))
    return loudness


def centred(own_key, shape, scale, limit, cuts=(), held_as=jnp.bfloat16):
    entries = scale * jax.random.normal(own_key, shape, jnp.float32)
    if cuts:
        entries = entries * steps_of(own_key, shape, cuts, -0.22, 0.18)
    return jnp.clip(entries, -limit, limit).astype(held_as)


def setup_inputs(seed: int = 0, part: int = 0) -> dict:
    key_list = jax.random.split(jax.random.key(seed), 6)
    part_keys = jax.random.split(jax.random.fold_in(key_list[5], part), 6)
    return {
        "residual": centred(part_keys[0], (TILES, C, HEIGHT, COLS), 1.0, 6.0, ((0, 4), (2, 2)), jnp.float32),
        "coefficients": centred(part_keys[1], (TILES, BLOCKS, KB, HEIGHT, COLS), 1.0, 6.0, ((0, 4), (2, 2), (3, 2))),
        "filter_store": draw_filter_store(jax.random.fold_in(jax.random.fold_in(key_list[5], part), 71), part),
        "plan": jax.random.randint(key_list[3], (STEPS,), 0, BLOCKS).astype(jnp.int32),
        "owner": draw_owner(jax.random.fold_in(key_list[5], 71), part),
    }


COEFF_STEP = 0.5
THRESHOLD = 0.3
FILTER_STEP = 40.0

def correlate(inputs, weights, pads):
    return lax.conv_general_dilated(inputs, weights, (1, 1), pads, dimension_numbers=('NCHW', 'OIHW', 'NCHW'), precision=lax.Precision.HIGHEST, preferred_element_type=jnp.float32)

def round_trip(values):
    return lax.optimization_barrier(values.astype(jnp.bfloat16)).astype(jnp.float32)

def reference(residual, coefficients, filter_store, plan, owner):
    scaling = FEAT ** (-0.5)
    pixel_total = float(TILES * HEIGHT * COLS)
    current = residual
    coeffs = coefficients
    store = filter_store
    updated = []
    for step_index in range(STEPS):
        block = plan[step_index].astype(jnp.int32)
        holder = owner[block].astype(jnp.int32)
        master = lax.dynamic_index_in_dim(store, holder, 0, keepdims=False)
        kernel = round_trip(master).reshape(KB, C, PATCH, PATCH)
        previous = lax.dynamic_index_in_dim(coeffs, block, 1, keepdims=False)
        previous_wide = previous.astype(jnp.float32)
        adjoint = scaling * correlate(round_trip(current), kernel[:, :, ::-1, ::-1], ((7, 8), (7, 8)))
        shifted = previous_wide - COEFF_STEP * adjoint
        fresh = (jnp.sign(shifted) * jnp.maximum(jnp.abs(shifted) - THRESHOLD, 0.0)).astype(jnp.bfloat16)
        fresh_wide = lax.optimization_barrier(fresh).astype(jnp.float32)
        change = round_trip(fresh_wide - previous_wide)
        synthesis = correlate(change, kernel.transpose(1, 0, 2, 3), ((8, 7), (8, 7)))
        current = current + scaling * synthesis
        target = round_trip(current)

        def synth_map(weights):
            return correlate(fresh_wide, weights, ((8, 7), (8, 7)))
        outputs, pullback = jax.vjp(synth_map, kernel.transpose(1, 0, 2, 3))
        grads = pullback(target)[0].transpose(1, 0, 2, 3).reshape(KB, FEAT)
        moved = master - FILTER_STEP * grads / pixel_total
        length = jnp.sqrt(lax.optimization_barrier(jnp.sum(moved * moved, axis=1, keepdims=True))) * scaling
        final = moved / jnp.maximum(length, 1.0)
        store = lax.dynamic_update_index_in_dim(store, final, holder, 0)
        coeffs = lax.dynamic_update_index_in_dim(coeffs, fresh, block, 1)
        updated.append(fresh)
    return (current, jnp.stack(updated, axis=1), store)
```

```python
import functools

import jax
import jax.numpy as jnp
from jax import lax
from jax.experimental import pallas as pl
from jax.experimental.pallas import tpu as pltpu
from jax.sharding import PartitionSpec as P

C = 8
PATCH = 16
STEPS = 2
ROWS = 32
COLS = 128
FEAT = 2048
HALO = 8
PADDED = ROWS + 2 * HALO
HALF = ROWS // 2
QC = PATCH * C

COEFF_STEP = 0.5
THRESHOLD = 0.3
FILTER_STEP = 40.0

BF16 = jnp.bfloat16
F32 = jnp.float32
VMEM_LIMIT = 40 * 1024 * 1024


def call(body, out_shape, scratch, flops, args):
    return pl.pallas_call(
        body,
        out_shape=out_shape,
        in_specs=[pl.BlockSpec(memory_space=pltpu.VMEM)] * len(args),
        out_specs=jax.tree.map(lambda _: pl.BlockSpec(memory_space=pltpu.VMEM), out_shape),
        scratch_shapes=scratch,
        compiler_params=pltpu.CompilerParams(vmem_limit_bytes=VMEM_LIMIT),
        cost_estimate=pl.CostEstimate(flops=flops, bytes_accessed=2 << 20, transcendentals=0),
    )(*args)


def shifted_rows(x, lanes):
    pieces = []
    for q in range(PATCH):
        moved = pltpu.roll(x, (q - HALO) % COLS, 1) if q != HALO else x
        source = lanes - (q - HALO)
        pieces.append(jnp.where((source >= 0) & (source < COLS), moved, 0.0))
    return jnp.concatenate(pieces, axis=0).astype(BF16)


def adjoint_body(count, x_ref, w_ref, prev_ref, fresh_ref, change_ref, xq):
    lanes = lax.broadcasted_iota(jnp.int32, (C, COLS), 1)

    def spread(r, carry):
        xq[pl.ds(pl.multiple_of(r * QC, QC), QC), :] = shifted_rows(x_ref[r], lanes)
        return carry

    lax.fori_loop(0, PADDED, spread, 0)
    depth = PATCH * QC

    def row_pair(i, carry):
        upper = xq[pl.ds(pl.multiple_of((i + 1) * QC, QC), depth), :]
        lower = xq[pl.ds(pl.multiple_of((i + 1 + HALF) * QC, QC), depth), :]
        both = jnp.concatenate([upper, lower], axis=1)
        sums = jnp.dot(w_ref[...], both, preferred_element_type=F32)
        for at in range(2):
            row = i + at * HALF
            before = prev_ref[row].astype(F32)
            adjoint = FEAT ** (-0.5) * sums[:, at * COLS : (at + 1) * COLS]
            v = before - COEFF_STEP * adjoint
            soft = jnp.where(v > THRESHOLD, v - THRESHOLD, jnp.where(v < -THRESHOLD, v + THRESHOLD, 0.0))
            fresh = soft.astype(BF16)
            fresh_ref[row] = fresh
            change_ref[row] = (fresh.astype(F32) - before).astype(BF16)
        return carry

    lax.fori_loop(0, HALF, row_pair, 0)


def fill(padded, before_ref, main_ref, after_ref, count):
    edge = HALO * count
    padded[0:edge, :] = before_ref[...]
    padded[edge : edge + ROWS * count, :] = main_ref[...]
    padded[edge + ROWS * count : 2 * edge + ROWS * count, :] = after_ref[...]


def synthesis_body(count, w_ref, before_ref, main_ref, after_ref, out_ref, padded, v_ref):
    lanes = lax.broadcasted_iota(jnp.int32, (C, COLS), 1)
    fill(padded, before_ref, main_ref, after_ref, count)
    group = COLS // count
    for base in range(0, PATCH, group):
        blocks = []
        for p in range(base, base + group):
            m = PATCH - 1 - p
            blocks.append(w_ref[:, m * QC : (m + 1) * QC].astype(F32))
        stacked = jnp.concatenate(blocks, axis=0)
        v_ref[:, base * count : (base + group) * count] = stacked.T.astype(BF16)
    depth = PATCH * count

    def row_pair(i, carry):
        upper = padded[pl.ds(pl.multiple_of(i * count, count), depth), :]
        lower = padded[pl.ds(pl.multiple_of((i + HALF) * count, count), depth), :]
        both = jnp.concatenate([upper, lower], axis=1)
        z = jnp.dot(v_ref[...], both, preferred_element_type=F32)
        for at in range(2):
            total = jnp.zeros((C, COLS), F32)
            for q in range(PATCH):
                part = z[q * C : (q + 1) * C, at * COLS : (at + 1) * COLS]
                moved = pltpu.roll(part, (HALO - q) % COLS, 1) if q != HALO else part
                source = lanes + (q - HALO)
                total = total + jnp.where((source >= 0) & (source < COLS), moved, 0.0)
            out_ref[i + at * HALF] = total.astype(BF16)
        return carry

    lax.fori_loop(0, HALF, row_pair, 0)


def gradient_body(count, x_ref, before_ref, main_ref, after_ref, out_ref, padded, total):
    lanes = lax.broadcasted_iota(jnp.int32, (C, COLS), 1)
    fill(padded, before_ref, main_ref, after_ref, count)
    total[...] = jnp.zeros_like(total)
    depth = PATCH * count

    def row_pair(i, carry):
        upper = padded[pl.ds(pl.multiple_of(i * count, count), depth), :]
        lower = padded[pl.ds(pl.multiple_of((i + HALF) * count, count), depth), :]
        both = jnp.concatenate([upper, lower], axis=1)
        target = jnp.concatenate([shifted_rows(x_ref[i], lanes), shifted_rows(x_ref[i + HALF], lanes)], axis=1)
        total[...] += lax.dot_general(both, target, (((1,), (1,)), ((), ())), preferred_element_type=F32)
        return carry

    lax.fori_loop(0, HALF, row_pair, 0)
    for p in range(PATCH):
        out_ref[:, p * QC : (p + 1) * QC] = total[p * count : (p + 1) * count, :]


def swap_halo(x, place):
    send = jnp.where(place == 0, x[ROWS - HALO :], x[:HALO])
    got = lax.ppermute(send, "sub", [(0, 1), (1, 0)])
    empty = jnp.zeros_like(got)
    return jnp.where(place == 1, got, empty), jnp.where(place == 0, got, empty)


def per_device(residual, coefficients, filter_store, plan, owner):
    scaling = FEAT ** (-0.5)
    sub_place = lax.axis_index("sub")
    tile_place = lax.axis_index("tile")
    pixel_total = float(lax.axis_size("tile") * lax.axis_size("sub") * ROWS * COLS)
    slot_count, count = filter_store.shape[:2]
    holders = [owner[plan[s]] for s in range(STEPS)]
    macs = 2 * count * FEAT * ROWS * COLS

    def picked(store, s):
        return lax.dynamic_index_in_dim(store, holders[s] % slot_count, 0, keepdims=False)

    def shared(stores):
        sent = [
            jnp.where(tile_place == holders[s] // slot_count, picked(store, s).astype(BF16), jnp.zeros((), BF16))
            for s, store in stores
        ]
        whole = lax.psum(jnp.stack(sent), "tile")
        cut = whole.reshape(-1, count, C, PATCH, PATCH)[:, :, :, ::-1]
        return cut.transpose(0, 1, 3, 4, 2).reshape(-1, count, FEAT)

    def updated(store, s, grads):
        master = picked(store, s)
        moved = master - FILTER_STEP * grads / pixel_total
        length = jnp.sqrt(jnp.sum(moved * moved, axis=1, keepdims=True)) * scaling
        final = moved / jnp.maximum(length, 1.0)
        written = lax.dynamic_update_index_in_dim(store, final, holders[s] % slot_count, 0)
        return jnp.where(tile_place == holders[s] // slot_count, written, store)

    def summed(local):
        whole = lax.psum(local, ("tile", "sub"))
        return whole.reshape(count, PATCH, PATCH, C).transpose(0, 3, 1, 2).reshape(count, FEAT)

    current = residual[0].transpose(1, 0, 2)
    first_pair = shared([(0, filter_store), (1, filter_store)])
    weights = first_pair[0]
    fresh_maps, local_grads, sums = [], [], []
    same = plan[0] == plan[1]
    for s in range(STEPS):
        previous = lax.dynamic_index_in_dim(coefficients[0], plan[s], 0, keepdims=False).transpose(1, 0, 2)
        if s == 1:
            previous = jnp.where(same, fresh_maps[0], previous)
            weights = lax.cond(
                same,
                lambda local, pair: shared([(1, updated(filter_store, 0, summed(local)))])[0],
                lambda local, pair: pair[1],
                local_grads[0],
                first_pair,
            )
        rounded = current.astype(BF16)
        before, after = swap_halo(rounded, sub_place)
        padded = jnp.concatenate([before, rounded, after], axis=0).astype(F32)
        maps = jax.ShapeDtypeStruct((ROWS, count, COLS), BF16)
        fresh, change = call(
            functools.partial(adjoint_body, count),
            (maps, maps),
            [pltpu.VMEM((PADDED * QC, COLS), BF16)],
            macs,
            (padded, weights, previous),
        )
        edges = swap_halo(jnp.stack([change, fresh], axis=1), sub_place)
        flat = lambda x: x.reshape(-1, COLS)
        space = pltpu.VMEM((PADDED * count, COLS), BF16)
        partial_sum = call(
            functools.partial(synthesis_body, count),
            jax.ShapeDtypeStruct((ROWS, C, COLS), BF16),
            [space, pltpu.VMEM((QC, PATCH * count), BF16)],
            macs,
            (weights, flat(edges[0][:, 0]), flat(change), flat(edges[1][:, 0])),
        )
        if lax.axis_size("chan") == 2:
            other = lax.ppermute(partial_sum, "chan", [(0, 1), (1, 0)])
            total = partial_sum.astype(F32) + other.astype(F32)
        else:
            total = lax.psum(partial_sum, "chan").astype(F32)
        current = current + scaling * total
        target = current.astype(BF16).astype(F32)
        local = call(
            functools.partial(gradient_body, count),
            jax.ShapeDtypeStruct((count, FEAT), F32),
            [space, pltpu.VMEM((PATCH * count, QC), F32)],
            macs,
            (target, flat(edges[0][:, 1]), flat(fresh), flat(edges[1][:, 1])),
        )
        fresh_maps.append(fresh)
        local_grads.append(local)
        sums.append(summed(local))
    store = filter_store
    for s in range(STEPS):
        store = updated(store, s, sums[s])
    coeffs_out = jnp.stack(fresh_maps, axis=0).transpose(0, 2, 1, 3)
    return (current.transpose(1, 0, 2)[None], coeffs_out[None], store)


def solution(mesh):
    placed = (
        P(("groups", "tile"), None, "sub", None),
        P(("groups", "tile"), None, "chan", "sub", None),
        P(("groups", "tile"), "chan", None),
        P(),
        P(),
    )
    return jax.shard_map(
        per_device,
        mesh=mesh,
        in_specs=placed,
        out_specs=(
            P(("groups", "tile"), None, "sub", None),
            P(("groups", "tile"), None, "chan", "sub", None),
            P(("groups", "tile"), "chan", None),
        ),
        check_vma=False,
    )
```

```python
import functools

import jax
import jax.numpy as jnp
from jax import lax
from jax.experimental import pallas as pl
from jax.experimental.pallas import tpu as pltpu
from jax.sharding import PartitionSpec as P

C = 8
PATCH = 16
STEPS = 2
ROWS = 32
COLS = 128
FEAT = 2048
HALO = 8
PADDED = ROWS + 2 * HALO
HALF = ROWS // 2
QC = PATCH * C

COEFF_STEP = 0.5
THRESHOLD = 0.3
FILTER_STEP = 40.0

BF16 = jnp.bfloat16
F32 = jnp.float32
VMEM_LIMIT = 40 * 1024 * 1024
MESH = pl.DeviceIdType.MESH


def call(body, out_shape, scratch, flops, args):
    return pl.pallas_call(
        body,
        out_shape=out_shape,
        in_specs=[pl.BlockSpec(memory_space=pltpu.VMEM)] * len(args),
        out_specs=jax.tree.map(lambda _: pl.BlockSpec(memory_space=pltpu.VMEM), out_shape),
        scratch_shapes=scratch,
        compiler_params=pltpu.CompilerParams(vmem_limit_bytes=VMEM_LIMIT),
        cost_estimate=pl.CostEstimate(flops=flops, bytes_accessed=2 << 20, transcendentals=0),
    )(*args)


def shifted_rows(x, lanes):
    pieces = []
    for q in range(PATCH):
        moved = pltpu.roll(x, (q - HALO) % COLS, 1) if q != HALO else x
        source = lanes - (q - HALO)
        pieces.append(jnp.where((source >= 0) & (source < COLS), moved, 0.0))
    return jnp.concatenate(pieces, axis=0).astype(BF16)


def adjoint_body(count, x_ref, w_ref, prev_ref, fresh_ref, change_ref, xq):
    lanes = lax.broadcasted_iota(jnp.int32, (C, COLS), 1)

    def spread(r, carry):
        xq[pl.ds(pl.multiple_of(r * QC, QC), QC), :] = shifted_rows(x_ref[r], lanes)
        return carry

    lax.fori_loop(0, PADDED, spread, 0)
    depth = PATCH * QC

    def row_pair(i, carry):
        upper = xq[pl.ds(pl.multiple_of((i + 1) * QC, QC), depth), :]
        lower = xq[pl.ds(pl.multiple_of((i + 1 + HALF) * QC, QC), depth), :]
        both = jnp.concatenate([upper, lower], axis=1)
        sums = jnp.dot(w_ref[...], both, preferred_element_type=F32)
        for at in range(2):
            row = i + at * HALF
            before = prev_ref[row].astype(F32)
            adjoint = FEAT ** (-0.5) * sums[:, at * COLS : (at + 1) * COLS]
            v = before - COEFF_STEP * adjoint
            soft = jnp.where(v > THRESHOLD, v - THRESHOLD, jnp.where(v < -THRESHOLD, v + THRESHOLD, 0.0))
            fresh = soft.astype(BF16)
            fresh_ref[row] = fresh
            change_ref[row] = (fresh.astype(F32) - before).astype(BF16)
        return carry

    lax.fori_loop(0, HALF, row_pair, 0)


def fill(padded, before_ref, main_ref, after_ref, count):
    edge = HALO * count
    padded[0:edge, :] = before_ref[...]
    padded[edge : edge + ROWS * count, :] = main_ref[...]
    padded[edge + ROWS * count : 2 * edge + ROWS * count, :] = after_ref[...]


def synthesis_body(count, w_ref, before_ref, main_ref, after_ref, out_ref, padded, v_ref):
    lanes = lax.broadcasted_iota(jnp.int32, (C, COLS), 1)
    fill(padded, before_ref, main_ref, after_ref, count)
    group = COLS // count
    for base in range(0, PATCH, group):
        blocks = []
        for p in range(base, base + group):
            m = PATCH - 1 - p
            blocks.append(w_ref[:, m * QC : (m + 1) * QC].astype(F32))
        stacked = jnp.concatenate(blocks, axis=0)
        v_ref[:, base * count : (base + group) * count] = stacked.T.astype(BF16)
    depth = PATCH * count

    def row_pair(i, carry):
        upper = padded[pl.ds(pl.multiple_of(i * count, count), depth), :]
        lower = padded[pl.ds(pl.multiple_of((i + HALF) * count, count), depth), :]
        both = jnp.concatenate([upper, lower], axis=1)
        z = jnp.dot(v_ref[...], both, preferred_element_type=F32)
        for at in range(2):
            total = jnp.zeros((C, COLS), F32)
            for q in range(PATCH):
                part = z[q * C : (q + 1) * C, at * COLS : (at + 1) * COLS]
                moved = pltpu.roll(part, (HALO - q) % COLS, 1) if q != HALO else part
                source = lanes + (q - HALO)
                total = total + jnp.where((source >= 0) & (source < COLS), moved, 0.0)
            out_ref[i + at * HALF] = total.astype(BF16)
        return carry

    lax.fori_loop(0, HALF, row_pair, 0)


def gradient_body(count, x_ref, before_ref, main_ref, after_ref, out_ref, padded, total):
    lanes = lax.broadcasted_iota(jnp.int32, (C, COLS), 1)
    fill(padded, before_ref, main_ref, after_ref, count)
    total[...] = jnp.zeros_like(total)
    depth = PATCH * count

    def row_pair(i, carry):
        upper = padded[pl.ds(pl.multiple_of(i * count, count), depth), :]
        lower = padded[pl.ds(pl.multiple_of((i + HALF) * count, count), depth), :]
        both = jnp.concatenate([upper, lower], axis=1)
        target = jnp.concatenate([shifted_rows(x_ref[i], lanes), shifted_rows(x_ref[i + HALF], lanes)], axis=1)
        total[...] += lax.dot_general(both, target, (((1,), (1,)), ((), ())), preferred_element_type=F32)
        return carry

    lax.fori_loop(0, HALF, row_pair, 0)
    for p in range(PATCH):
        out_ref[:, p * QC : (p + 1) * QC] = total[p * count : (p + 1) * count, :]


def tile_sum_body(count, paired, x_ref, out_ref, *scratch):
    got, mine, send_sems, recv_sems = scratch[:4]
    me = lax.axis_index("tile")
    half = lax.axis_index("sub")
    peers = [lax.rem(me + d, count) for d in range(1, count)]
    barrier = pltpu.get_barrier_semaphore()
    for peer in peers:
        pl.semaphore_signal(barrier, inc=1, device_id={"tile": peer}, device_id_type=MESH)
    pl.semaphore_signal(barrier, inc=1, device_id={"sub": 1 - half}, device_id_type=MESH)
    pl.semaphore_wait(barrier, count)

    def remote(src, dst, at, where):
        return pltpu.make_async_remote_copy(
            src_ref=src,
            dst_ref=dst,
            send_sem=send_sems.at[at],
            recv_sem=recv_sems.at[at],
            device_id=where,
            device_id_type=MESH,
        )

    if paired:
        other = scratch[4]
        cross = remote(x_ref.at[1 - half], other, 3 * count, {"sub": 1 - half})
        cross.start()
        cross.wait()
        for part in range(count):
            mine[part] = (x_ref[half, part] + other[part]).astype(BF16)
    scattered = []
    for d, peer in enumerate(peers):
        source = mine.at[peer] if paired else x_ref.at[half, peer]
        copy = remote(source, got.at[d], d, {"tile": peer})
        copy.start()
        scattered.append(copy)
    if paired:
        total = x_ref[half, me] + other[me]
    else:
        total = x_ref[half, me].astype(F32)
    for d, copy in enumerate(scattered):
        copy.wait_recv()
        total = total + got[d].astype(F32)
    out_ref[half, me] = total.astype(BF16)
    gathered, crossed = [], []
    for d, peer in enumerate(peers):
        copy = remote(out_ref.at[half, me], out_ref.at[half, me], count + d, {"tile": peer})
        copy.start()
        gathered.append(copy)

    def forward(at, part):
        copy = remote(out_ref.at[half, part], out_ref.at[half, part], at, {"sub": 1 - half})
        copy.start()
        crossed.append(copy)

    forward(2 * count, me)
    for d, copy in enumerate(gathered):
        copy.wait_recv()
        forward(2 * count + 1 + d, lax.rem(me + count - 1 - d, count))
    for copy in scattered + gathered:
        copy.wait_send()
    for copy in crossed:
        copy.wait()


def tile_sum(x, paired, ident):
    count = lax.axis_size("tile")
    wide = x.size // (2 * count * 16)
    if wide < COLS or lax.axis_size("sub") != 2:
        return lax.psum(x, ("tile", "sub") if paired else "tile")
    block = (count, 16, wide)
    scratch = [
        pltpu.VMEM((count - 1, 16, wide), BF16),
        pltpu.VMEM(block, BF16),
        pltpu.SemaphoreType.DMA((3 * count + 1,)),
        pltpu.SemaphoreType.DMA((3 * count + 1,)),
    ]
    if paired:
        scratch.append(pltpu.VMEM(block, F32))
    out = pl.pallas_call(
        functools.partial(tile_sum_body, count, paired),
        out_shape=jax.ShapeDtypeStruct((2,) + block, BF16),
        in_specs=[pl.BlockSpec(memory_space=pltpu.VMEM)],
        out_specs=pl.BlockSpec(memory_space=pltpu.VMEM),
        scratch_shapes=scratch,
        compiler_params=pltpu.CompilerParams(
            collective_id=ident, has_side_effects=True, vmem_limit_bytes=VMEM_LIMIT
        ),
    )(x.reshape((2,) + block))
    return out.reshape(x.shape)


def swap_halo(x, place):
    send = jnp.where(place == 0, x[ROWS - HALO :], x[:HALO])
    got = lax.ppermute(send, "sub", [(0, 1), (1, 0)])
    empty = jnp.zeros_like(got)
    return jnp.where(place == 1, got, empty), jnp.where(place == 0, got, empty)


def per_device(residual, coefficients, filter_store, plan, owner):
    scaling = FEAT ** (-0.5)
    sub_place = lax.axis_index("sub")
    tile_place = lax.axis_index("tile")
    pixel_total = float(lax.axis_size("tile") * lax.axis_size("sub") * ROWS * COLS)
    slot_count, count = filter_store.shape[:2]
    holders = [owner[plan[s]] for s in range(STEPS)]
    macs = 2 * count * FEAT * ROWS * COLS

    def picked(store, s):
        return lax.dynamic_index_in_dim(store, holders[s] % slot_count, 0, keepdims=False)

    def shared(stores, ident):
        sent = [
            jnp.where(tile_place == holders[s] // slot_count, picked(store, s).astype(BF16), jnp.zeros((), BF16))
            for s, store in stores
        ]
        whole = tile_sum(jnp.stack(sent), False, ident)
        cut = whole.reshape(-1, count, C, PATCH, PATCH)[:, :, :, ::-1]
        return cut.transpose(0, 1, 3, 4, 2).reshape(-1, count, FEAT)

    def updated(store, s, grads):
        master = picked(store, s)
        moved = master - FILTER_STEP * grads / pixel_total
        length = jnp.sqrt(jnp.sum(moved * moved, axis=1, keepdims=True)) * scaling
        final = moved / jnp.maximum(length, 1.0)
        written = lax.dynamic_update_index_in_dim(store, final, holders[s] % slot_count, 0)
        return jnp.where(tile_place == holders[s] // slot_count, written, store)

    def summed(local, ident):
        whole = tile_sum(jnp.stack(local), True, ident).astype(F32)
        return whole.reshape(-1, count, PATCH, PATCH, C).transpose(0, 1, 4, 2, 3).reshape(-1, count, FEAT)

    current = residual[0].transpose(1, 0, 2)
    first_pair = shared([(0, filter_store), (1, filter_store)], 0)
    weights = first_pair[0]
    fresh_maps, local_grads = [], []
    same = plan[0] == plan[1]
    for s in range(STEPS):
        previous = lax.dynamic_index_in_dim(coefficients[0], plan[s], 0, keepdims=False).transpose(1, 0, 2)
        if s == 1:
            previous = jnp.where(same, fresh_maps[0], previous)
            weights = lax.cond(
                same,
                lambda local, pair: shared([(1, updated(filter_store, 0, summed([local], 2)[0]))], 3)[0],
                lambda local, pair: pair[1],
                local_grads[0],
                first_pair,
            )
        rounded = current.astype(BF16)
        before, after = swap_halo(rounded, sub_place)
        padded = jnp.concatenate([before, rounded, after], axis=0).astype(F32)
        maps = jax.ShapeDtypeStruct((ROWS, count, COLS), BF16)
        fresh, change = call(
            functools.partial(adjoint_body, count),
            (maps, maps),
            [pltpu.VMEM((PADDED * QC, COLS), BF16)],
            macs,
            (padded, weights, previous),
        )
        edges = swap_halo(jnp.stack([change, fresh], axis=1), sub_place)
        flat = lambda x: x.reshape(-1, COLS)
        space = pltpu.VMEM((PADDED * count, COLS), BF16)
        partial_sum = call(
            functools.partial(synthesis_body, count),
            jax.ShapeDtypeStruct((ROWS, C, COLS), BF16),
            [space, pltpu.VMEM((QC, PATCH * count), BF16)],
            macs,
            (weights, flat(edges[0][:, 0]), flat(change), flat(edges[1][:, 0])),
        )
        if lax.axis_size("chan") == 2:
            other = lax.ppermute(partial_sum, "chan", [(0, 1), (1, 0)])
            total = partial_sum.astype(F32) + other.astype(F32)
        else:
            total = lax.psum(partial_sum, "chan").astype(F32)
        current = current + scaling * total
        target = current.astype(BF16).astype(F32)
        local = call(
            functools.partial(gradient_body, count),
            jax.ShapeDtypeStruct((count, FEAT), F32),
            [space, pltpu.VMEM((PATCH * count, QC), F32)],
            macs,
            (target, flat(edges[0][:, 1]), flat(fresh), flat(edges[1][:, 1])),
        )
        fresh_maps.append(fresh)
        local_grads.append(local)
    sums = summed(local_grads, 1)
    store = filter_store
    for s in range(STEPS):
        store = updated(store, s, sums[s])
    coeffs_out = jnp.stack(fresh_maps, axis=0).transpose(0, 2, 1, 3)
    return (current.transpose(1, 0, 2)[None], coeffs_out[None], store)


def solution(mesh):
    placed = (
        P(("groups", "tile"), None, "sub", None),
        P(("groups", "tile"), None, "chan", "sub", None),
        P(("groups", "tile"), "chan", None),
        P(),
        P(),
    )
    return jax.shard_map(
        per_device,
        mesh=mesh,
        in_specs=placed,
        out_specs=(
            P(("groups", "tile"), None, "sub", None),
            P(("groups", "tile"), None, "chan", "sub", None),
            P(("groups", "tile"), "chan", None),
        ),
        check_vma=False,
    )
```

```python
import functools

import jax
import jax.numpy as jnp
from jax import lax
from jax.experimental import pallas as pl
from jax.experimental.pallas import tpu as pltpu
from jax.sharding import PartitionSpec as P

C = 8
PATCH = 16
STEPS = 2
ROWS = 32
COLS = 128
FEAT = 2048
HALO = 8
PADDED = ROWS + 2 * HALO
HALF = ROWS // 2
QC = PATCH * C

COEFF_STEP = 0.5
THRESHOLD = 0.3
FILTER_STEP = 40.0

BF16 = jnp.bfloat16
F32 = jnp.float32
VMEM_LIMIT = 40 * 1024 * 1024
MESH = pl.DeviceIdType.MESH


def call(body, out_shape, scratch, flops, args):
    return pl.pallas_call(
        body,
        out_shape=out_shape,
        in_specs=[pl.BlockSpec(memory_space=pltpu.VMEM)] * len(args),
        out_specs=jax.tree.map(lambda _: pl.BlockSpec(memory_space=pltpu.VMEM), out_shape),
        scratch_shapes=scratch,
        compiler_params=pltpu.CompilerParams(vmem_limit_bytes=VMEM_LIMIT),
        cost_estimate=pl.CostEstimate(flops=flops, bytes_accessed=2 << 20, transcendentals=0),
    )(*args)


def shifted_rows(x, lanes):
    pieces = []
    for q in range(PATCH):
        moved = pltpu.roll(x, (q - HALO) % COLS, 1) if q != HALO else x
        source = lanes - (q - HALO)
        pieces.append(jnp.where((source >= 0) & (source < COLS), moved, 0.0))
    return jnp.concatenate(pieces, axis=0).astype(BF16)


def adjoint_body(count, x_ref, w_ref, prev_ref, fresh_ref, change_ref, xq):
    lanes = lax.broadcasted_iota(jnp.int32, (C, COLS), 1)

    def spread(r, carry):
        xq[pl.ds(pl.multiple_of(r * QC, QC), QC), :] = shifted_rows(x_ref[r], lanes)
        return carry

    lax.fori_loop(0, PADDED, spread, 0)
    depth = PATCH * QC

    def row_pair(i, carry):
        upper = xq[pl.ds(pl.multiple_of((i + 1) * QC, QC), depth), :]
        lower = xq[pl.ds(pl.multiple_of((i + 1 + HALF) * QC, QC), depth), :]
        both = jnp.concatenate([upper, lower], axis=1)
        sums = jnp.dot(w_ref[...], both, preferred_element_type=F32)
        for at in range(2):
            row = i + at * HALF
            before = prev_ref[row].astype(F32)
            adjoint = FEAT ** (-0.5) * sums[:, at * COLS : (at + 1) * COLS]
            v = before - COEFF_STEP * adjoint
            soft = jnp.where(v > THRESHOLD, v - THRESHOLD, jnp.where(v < -THRESHOLD, v + THRESHOLD, 0.0))
            fresh = soft.astype(BF16)
            fresh_ref[row] = fresh
            change_ref[row] = (fresh.astype(F32) - before).astype(BF16)
        return carry

    lax.fori_loop(0, HALF, row_pair, 0)


def fill(padded, before_ref, main_ref, after_ref, count):
    edge = HALO * count
    padded[0:edge, :] = before_ref[...]
    padded[edge : edge + ROWS * count, :] = main_ref[...]
    padded[edge + ROWS * count : 2 * edge + ROWS * count, :] = after_ref[...]


def synthesis_body(count, w_ref, before_ref, main_ref, after_ref, out_ref, padded, v_ref):
    lanes = lax.broadcasted_iota(jnp.int32, (C, COLS), 1)
    fill(padded, before_ref, main_ref, after_ref, count)
    group = COLS // count
    for base in range(0, PATCH, group):
        blocks = []
        for p in range(base, base + group):
            m = PATCH - 1 - p
            blocks.append(w_ref[:, m * QC : (m + 1) * QC].astype(F32))
        stacked = jnp.concatenate(blocks, axis=0)
        v_ref[:, base * count : (base + group) * count] = stacked.T.astype(BF16)
    depth = PATCH * count

    def row_pair(i, carry):
        upper = padded[pl.ds(pl.multiple_of(i * count, count), depth), :]
        lower = padded[pl.ds(pl.multiple_of((i + HALF) * count, count), depth), :]
        both = jnp.concatenate([upper, lower], axis=1)
        z = jnp.dot(v_ref[...], both, preferred_element_type=F32)
        for at in range(2):
            total = jnp.zeros((C, COLS), F32)
            for q in range(PATCH):
                part = z[q * C : (q + 1) * C, at * COLS : (at + 1) * COLS]
                moved = pltpu.roll(part, (HALO - q) % COLS, 1) if q != HALO else part
                source = lanes + (q - HALO)
                total = total + jnp.where((source >= 0) & (source < COLS), moved, 0.0)
            out_ref[i + at * HALF] = total.astype(BF16)
        return carry

    lax.fori_loop(0, HALF, row_pair, 0)


def gradient_body(count, x_ref, before_ref, main_ref, after_ref, out_ref, padded, total):
    lanes = lax.broadcasted_iota(jnp.int32, (C, COLS), 1)
    fill(padded, before_ref, main_ref, after_ref, count)
    total[...] = jnp.zeros_like(total)
    depth = PATCH * count

    def row_pair(i, carry):
        upper = padded[pl.ds(pl.multiple_of(i * count, count), depth), :]
        lower = padded[pl.ds(pl.multiple_of((i + HALF) * count, count), depth), :]
        both = jnp.concatenate([upper, lower], axis=1)
        target = jnp.concatenate([shifted_rows(x_ref[i], lanes), shifted_rows(x_ref[i + HALF], lanes)], axis=1)
        total[...] += lax.dot_general(both, target, (((1,), (1,)), ((), ())), preferred_element_type=F32)
        return carry

    lax.fori_loop(0, HALF, row_pair, 0)
    for p in range(PATCH):
        out_ref[:, p * QC : (p + 1) * QC] = total[p * count : (p + 1) * count, :]


def tile_sum_body(count, paired, x_ref, out_ref, *scratch):
    got, mine, send_sems, recv_sems = scratch[:4]
    me = lax.axis_index("tile")
    half = lax.axis_index("sub")
    peers = [lax.rem(me + d, count) for d in range(1, count)]
    barrier = pltpu.get_barrier_semaphore()
    for peer in peers:
        pl.semaphore_signal(barrier, inc=1, device_id={"tile": peer}, device_id_type=MESH)
    pl.semaphore_signal(barrier, inc=1, device_id={"sub": 1 - half}, device_id_type=MESH)
    pl.semaphore_wait(barrier, count)

    def remote(src, dst, at, where):
        return pltpu.make_async_remote_copy(
            src_ref=src,
            dst_ref=dst,
            send_sem=send_sems.at[at],
            recv_sem=recv_sems.at[at],
            device_id=where,
            device_id_type=MESH,
        )

    if paired:
        other = scratch[4]
        cross = remote(x_ref.at[1 - half], other, 3 * count, {"sub": 1 - half})
        cross.start()
        cross.wait()
        for part in range(count):
            mine[part] = (x_ref[half, part] + other[part]).astype(BF16)
    scattered = []
    for d, peer in enumerate(peers):
        source = mine.at[peer] if paired else x_ref.at[half, peer]
        copy = remote(source, got.at[d], d, {"tile": peer})
        copy.start()
        scattered.append(copy)
    if paired:
        total = x_ref[half, me] + other[me]
    else:
        total = x_ref[half, me].astype(F32)
    for d, copy in enumerate(scattered):
        copy.wait_recv()
        total = total + got[d].astype(F32)
    out_ref[half, me] = total.astype(BF16)
    gathered, crossed = [], []
    for d, peer in enumerate(peers):
        copy = remote(out_ref.at[half, me], out_ref.at[half, me], count + d, {"tile": peer})
        copy.start()
        gathered.append(copy)

    def forward(at, part):
        copy = remote(out_ref.at[half, part], out_ref.at[half, part], at, {"sub": 1 - half})
        copy.start()
        crossed.append(copy)

    forward(2 * count, me)
    for d, copy in enumerate(gathered):
        copy.wait_recv()
        forward(2 * count + 1 + d, lax.rem(me + count - 1 - d, count))
    for copy in scattered + gathered:
        copy.wait_send()
    for copy in crossed:
        copy.wait()


def tile_sum(x, paired, ident):
    count = lax.axis_size("tile")
    wide = x.size // (2 * count * 16)
    if wide < COLS or lax.axis_size("sub") != 2:
        return lax.psum(x, ("tile", "sub") if paired else "tile")
    block = (count, 16, wide)
    scratch = [
        pltpu.VMEM((count - 1, 16, wide), BF16),
        pltpu.VMEM(block, BF16),
        pltpu.SemaphoreType.DMA((3 * count + 1,)),
        pltpu.SemaphoreType.DMA((3 * count + 1,)),
    ]
    if paired:
        scratch.append(pltpu.VMEM(block, F32))
    out = pl.pallas_call(
        functools.partial(tile_sum_body, count, paired),
        out_shape=jax.ShapeDtypeStruct((2,) + block, BF16),
        in_specs=[pl.BlockSpec(memory_space=pltpu.VMEM)],
        out_specs=pl.BlockSpec(memory_space=pltpu.VMEM),
        scratch_shapes=scratch,
        compiler_params=pltpu.CompilerParams(
            collective_id=ident, has_side_effects=True, vmem_limit_bytes=VMEM_LIMIT
        ),
    )(x.reshape((2,) + block))
    return out.reshape(x.shape)


def prepare_body(slots, steps, here_ref, plan_ref, owner_ref, store_ref, out_ref, held, sems):
    copies = []
    for at, s in enumerate(steps):
        holder = owner_ref[plan_ref[s]]
        copy = pltpu.make_async_copy(store_ref.at[lax.rem(holder, slots)], held.at[at], sems.at[at])
        copy.start()
        copies.append((holder, copy))
    for at, (holder, copy) in enumerate(copies):
        copy.wait()
        mine = lax.div(holder, slots) == here_ref[0]

        @pl.when(mine)
        def _():
            out_ref[at] = held[at].astype(BF16)

        @pl.when(jnp.logical_not(mine))
        def _():
            out_ref[at] = jnp.zeros(out_ref.shape[1:], BF16)


def prepare(store, steps, plan, owner, here):
    slots, count = store.shape[:2]
    smem = pl.BlockSpec(memory_space=pltpu.SMEM)
    return pl.pallas_call(
        functools.partial(prepare_body, slots, steps),
        out_shape=jax.ShapeDtypeStruct((len(steps), count, FEAT), BF16),
        in_specs=[smem, smem, smem, pl.BlockSpec(memory_space=pl.ANY)],
        out_specs=pl.BlockSpec(memory_space=pltpu.VMEM),
        scratch_shapes=[pltpu.VMEM((len(steps), count, FEAT), F32), pltpu.SemaphoreType.DMA((len(steps),))],
        compiler_params=pltpu.CompilerParams(vmem_limit_bytes=VMEM_LIMIT),
    )(here.reshape(1), plan, owner, store)


def permutation():
    side = FEAT // 2
    rows = lax.broadcasted_iota(jnp.int32, (side, side), 0)
    cols = lax.broadcasted_iota(jnp.int32, (side, side), 1)
    source = (cols & 7) * 128 + (cols >> 7) * 16 + ((cols >> 3) & 15)
    return jnp.where(rows == source, 1.0, 0.0).astype(BF16)


def arrange_body(x_ref, out_ref):
    steps, count = x_ref.shape[:2]
    parts = []
    for s in range(steps):
        for high in range(2):
            pieces = [x_ref[s, :, c * 256 + high * 128 : c * 256 + high * 128 + 128] for c in range(C)]
            parts.append(jnp.concatenate(pieces, axis=1))
    moved = jnp.dot(jnp.concatenate(parts, axis=0), permutation(), preferred_element_type=F32).astype(BF16)
    for s in range(steps):
        for high in range(2):
            top = (2 * s + high) * count
            for r in range(8):
                m = PATCH - 1 - (high * 8 + r)
                out_ref[s, :, m * QC : (m + 1) * QC] = moved[top : top + count, r * QC : (r + 1) * QC]


def restore_body(x_ref, out_ref):
    steps, count = x_ref.shape[:2]
    side = FEAT // 2
    parts = [x_ref[s, :, high * side : (high + 1) * side] for s in range(steps) for high in range(2)]
    moved = lax.dot_general(
        jnp.concatenate(parts, axis=0).astype(BF16),
        permutation(),
        (((1,), (1,)), ((), ())),
        preferred_element_type=F32,
    )
    for s in range(steps):
        for high in range(2):
            top = (2 * s + high) * count
            for c in range(C):
                out_ref[s, :, c * 256 + high * 128 : c * 256 + high * 128 + 128] = moved[
                    top : top + count, c * 128 : c * 128 + 128
                ]


def swap_halo(x, place):
    send = jnp.where(place == 0, x[ROWS - HALO :], x[:HALO])
    got = lax.ppermute(send, "sub", [(0, 1), (1, 0)])
    empty = jnp.zeros_like(got)
    return jnp.where(place == 1, got, empty), jnp.where(place == 0, got, empty)


def per_device(residual, coefficients, filter_store, plan, owner):
    scaling = FEAT ** (-0.5)
    sub_place = lax.axis_index("sub")
    tile_place = lax.axis_index("tile")
    pixel_total = float(lax.axis_size("tile") * lax.axis_size("sub") * ROWS * COLS)
    slot_count, count = filter_store.shape[:2]
    holders = [owner[plan[s]] for s in range(STEPS)]
    macs = 2 * count * FEAT * ROWS * COLS

    def picked(store, s):
        return lax.dynamic_index_in_dim(store, holders[s] % slot_count, 0, keepdims=False)

    def shared(store, steps, ident):
        whole = tile_sum(prepare(store, steps, plan, owner, tile_place), False, ident)
        return call(arrange_body, jax.ShapeDtypeStruct(whole.shape, BF16), [], macs, (whole,))

    def updated(store, s, grads):
        master = picked(store, s)
        moved = master - FILTER_STEP * grads / pixel_total
        length = jnp.sqrt(jnp.sum(moved * moved, axis=1, keepdims=True)) * scaling
        final = moved / jnp.maximum(length, 1.0)
        written = lax.dynamic_update_index_in_dim(store, final, holders[s] % slot_count, 0)
        return jnp.where(tile_place == holders[s] // slot_count, written, store)

    def summed(local, ident):
        whole = tile_sum(jnp.stack(local), True, ident)
        return call(restore_body, jax.ShapeDtypeStruct(whole.shape, F32), [], macs, (whole,))

    current = residual[0].transpose(1, 0, 2)
    first_pair = shared(filter_store, (0, 1), 0)
    weights = first_pair[0]
    fresh_maps, local_grads = [], []
    same = plan[0] == plan[1]
    for s in range(STEPS):
        previous = lax.dynamic_index_in_dim(coefficients[0], plan[s], 0, keepdims=False).transpose(1, 0, 2)
        if s == 1:
            previous = jnp.where(same, fresh_maps[0], previous)
            weights = lax.cond(
                same,
                lambda local, pair: shared(updated(filter_store, 0, summed([local], 2)[0]), (1,), 3)[0],
                lambda local, pair: pair[1],
                local_grads[0],
                first_pair,
            )
        rounded = current.astype(BF16)
        before, after = swap_halo(rounded, sub_place)
        padded = jnp.concatenate([before, rounded, after], axis=0).astype(F32)
        maps = jax.ShapeDtypeStruct((ROWS, count, COLS), BF16)
        fresh, change = call(
            functools.partial(adjoint_body, count),
            (maps, maps),
            [pltpu.VMEM((PADDED * QC, COLS), BF16)],
            macs,
            (padded, weights, previous),
        )
        edges = swap_halo(jnp.stack([change, fresh], axis=1), sub_place)
        flat = lambda x: x.reshape(-1, COLS)
        space = pltpu.VMEM((PADDED * count, COLS), BF16)
        partial_sum = call(
            functools.partial(synthesis_body, count),
            jax.ShapeDtypeStruct((ROWS, C, COLS), BF16),
            [space, pltpu.VMEM((QC, PATCH * count), BF16)],
            macs,
            (weights, flat(edges[0][:, 0]), flat(change), flat(edges[1][:, 0])),
        )
        if lax.axis_size("chan") == 2:
            other = lax.ppermute(partial_sum, "chan", [(0, 1), (1, 0)])
            total = partial_sum.astype(F32) + other.astype(F32)
        else:
            total = lax.psum(partial_sum, "chan").astype(F32)
        current = current + scaling * total
        target = current.astype(BF16).astype(F32)
        local = call(
            functools.partial(gradient_body, count),
            jax.ShapeDtypeStruct((count, FEAT), F32),
            [space, pltpu.VMEM((PATCH * count, QC), F32)],
            macs,
            (target, flat(edges[0][:, 1]), flat(fresh), flat(edges[1][:, 1])),
        )
        fresh_maps.append(fresh)
        local_grads.append(local)
    sums = summed(local_grads, 1)
    store = filter_store
    for s in range(STEPS):
        store = updated(store, s, sums[s])
    coeffs_out = jnp.stack(fresh_maps, axis=0).transpose(0, 2, 1, 3)
    return (current.transpose(1, 0, 2)[None], coeffs_out[None], store)


def solution(mesh):
    placed = (
        P(("groups", "tile"), None, "sub", None),
        P(("groups", "tile"), None, "chan", "sub", None),
        P(("groups", "tile"), "chan", None),
        P(),
        P(),
    )
    return jax.shard_map(
        per_device,
        mesh=mesh,
        in_specs=placed,
        out_specs=(
            P(("groups", "tile"), None, "sub", None),
            P(("groups", "tile"), None, "chan", "sub", None),
            P(("groups", "tile"), "chan", None),
        ),
        check_vma=False,
    )
```

```python
import functools

import jax
import jax.numpy as jnp
from jax import lax
from jax.experimental import pallas as pl
from jax.experimental.pallas import tpu as pltpu
from jax.sharding import PartitionSpec as P

C = 8
PATCH = 16
STEPS = 2
ROWS = 32
COLS = 128
FEAT = 2048
HALO = 8
PADDED = ROWS + 2 * HALO
HALF = ROWS // 2
QC = PATCH * C

COEFF_STEP = 0.5
THRESHOLD = 0.3
FILTER_STEP = 40.0

BF16 = jnp.bfloat16
F32 = jnp.float32
VMEM_LIMIT = 40 * 1024 * 1024
MESH = pl.DeviceIdType.MESH


def call(body, out_shape, scratch, flops, args):
    return pl.pallas_call(
        body,
        out_shape=out_shape,
        in_specs=[pl.BlockSpec(memory_space=pltpu.VMEM)] * len(args),
        out_specs=jax.tree.map(lambda _: pl.BlockSpec(memory_space=pltpu.VMEM), out_shape),
        scratch_shapes=scratch,
        compiler_params=pltpu.CompilerParams(vmem_limit_bytes=VMEM_LIMIT),
        cost_estimate=pl.CostEstimate(flops=flops, bytes_accessed=2 << 20, transcendentals=0),
    )(*args)


def shifted_rows(x, lanes):
    pieces = []
    for q in range(PATCH):
        moved = pltpu.roll(x, (q - HALO) % COLS, 1) if q != HALO else x
        source = lanes - (q - HALO)
        pieces.append(jnp.where((source >= 0) & (source < COLS), moved, 0.0))
    return jnp.concatenate(pieces, axis=0).astype(BF16)


def adjoint_body(count, x_ref, w_ref, prev_ref, fresh_ref, change_ref, xq):
    lanes = lax.broadcasted_iota(jnp.int32, (C, COLS), 1)

    def spread(r, carry):
        xq[pl.ds(pl.multiple_of(r * QC, QC), QC), :] = shifted_rows(x_ref[r], lanes)
        return carry

    lax.fori_loop(0, PADDED, spread, 0)
    depth = PATCH * QC

    def row_pair(i, carry):
        upper = xq[pl.ds(pl.multiple_of((i + 1) * QC, QC), depth), :]
        lower = xq[pl.ds(pl.multiple_of((i + 1 + HALF) * QC, QC), depth), :]
        both = jnp.concatenate([upper, lower], axis=1)
        sums = jnp.dot(w_ref[...], both, preferred_element_type=F32)
        for at in range(2):
            row = i + at * HALF
            before = prev_ref[row].astype(F32)
            adjoint = FEAT ** (-0.5) * sums[:, at * COLS : (at + 1) * COLS]
            v = before - COEFF_STEP * adjoint
            soft = jnp.where(v > THRESHOLD, v - THRESHOLD, jnp.where(v < -THRESHOLD, v + THRESHOLD, 0.0))
            fresh = soft.astype(BF16)
            fresh_ref[row] = fresh
            change_ref[row] = (fresh.astype(F32) - before).astype(BF16)
        return carry

    lax.fori_loop(0, HALF, row_pair, 0)


def fill(padded, before_ref, main_ref, after_ref, count):
    edge = HALO * count
    padded[0:edge, :] = before_ref[...]
    padded[edge : edge + ROWS * count, :] = main_ref[...]
    padded[edge + ROWS * count : 2 * edge + ROWS * count, :] = after_ref[...]


def synthesis_body(count, w_ref, before_ref, main_ref, after_ref, out_ref, padded, v_ref):
    lanes = lax.broadcasted_iota(jnp.int32, (C, COLS), 1)
    fill(padded, before_ref, main_ref, after_ref, count)
    group = COLS // count
    for base in range(0, PATCH, group):
        blocks = []
        for p in range(base, base + group):
            m = PATCH - 1 - p
            blocks.append(w_ref[:, m * QC : (m + 1) * QC].astype(F32))
        stacked = jnp.concatenate(blocks, axis=0)
        v_ref[:, base * count : (base + group) * count] = stacked.T.astype(BF16)
    depth = PATCH * count

    def row_pair(i, carry):
        upper = padded[pl.ds(pl.multiple_of(i * count, count), depth), :]
        lower = padded[pl.ds(pl.multiple_of((i + HALF) * count, count), depth), :]
        both = jnp.concatenate([upper, lower], axis=1)
        z = jnp.dot(v_ref[...], both, preferred_element_type=F32)
        for at in range(2):
            total = jnp.zeros((C, COLS), F32)
            for q in range(PATCH):
                part = z[q * C : (q + 1) * C, at * COLS : (at + 1) * COLS]
                moved = pltpu.roll(part, (HALO - q) % COLS, 1) if q != HALO else part
                source = lanes + (q - HALO)
                total = total + jnp.where((source >= 0) & (source < COLS), moved, 0.0)
            out_ref[i + at * HALF] = total.astype(BF16)
        return carry

    lax.fori_loop(0, HALF, row_pair, 0)


def gradient_body(count, x_ref, before_ref, main_ref, after_ref, out_ref, padded, total):
    lanes = lax.broadcasted_iota(jnp.int32, (C, COLS), 1)
    fill(padded, before_ref, main_ref, after_ref, count)
    total[...] = jnp.zeros_like(total)
    depth = PATCH * count

    def row_pair(i, carry):
        upper = padded[pl.ds(pl.multiple_of(i * count, count), depth), :]
        lower = padded[pl.ds(pl.multiple_of((i + HALF) * count, count), depth), :]
        both = jnp.concatenate([upper, lower], axis=1)
        target = jnp.concatenate([shifted_rows(x_ref[i], lanes), shifted_rows(x_ref[i + HALF], lanes)], axis=1)
        total[...] += lax.dot_general(both, target, (((1,), (1,)), ((), ())), preferred_element_type=F32)
        return carry

    lax.fori_loop(0, HALF, row_pair, 0)
    for p in range(PATCH):
        out_ref[:, p * QC : (p + 1) * QC] = total[p * count : (p + 1) * count, :]


def tile_sum_body(count, paired, x_ref, out_ref, *scratch):
    got, mine, send_sems, recv_sems = scratch[:4]
    me = lax.axis_index("tile")
    half = lax.axis_index("sub")
    peers = [lax.rem(me + d, count) for d in range(1, count)]
    barrier = pltpu.get_barrier_semaphore()
    for peer in peers:
        pl.semaphore_signal(barrier, inc=1, device_id={"tile": peer}, device_id_type=MESH)
    pl.semaphore_signal(barrier, inc=1, device_id={"sub": 1 - half}, device_id_type=MESH)
    pl.semaphore_wait(barrier, count)

    def remote(src, dst, at, where):
        return pltpu.make_async_remote_copy(
            src_ref=src,
            dst_ref=dst,
            send_sem=send_sems.at[at],
            recv_sem=recv_sems.at[at],
            device_id=where,
            device_id_type=MESH,
        )

    if paired:
        other = scratch[4]
        cross = remote(x_ref.at[1 - half], other, 3 * count, {"sub": 1 - half})
        cross.start()
        cross.wait()
        for part in range(count):
            mine[part] = (x_ref[half, part] + other[part]).astype(BF16)
    scattered = []
    for d, peer in enumerate(peers):
        source = mine.at[peer] if paired else x_ref.at[half, peer]
        copy = remote(source, got.at[d], d, {"tile": peer})
        copy.start()
        scattered.append(copy)
    if paired:
        total = x_ref[half, me] + other[me]
    else:
        total = x_ref[half, me].astype(F32)
    for d, copy in enumerate(scattered):
        copy.wait_recv()
        total = total + got[d].astype(F32)
    out_ref[half, me] = total.astype(BF16)
    gathered, crossed = [], []
    for d, peer in enumerate(peers):
        copy = remote(out_ref.at[half, me], out_ref.at[half, me], count + d, {"tile": peer})
        copy.start()
        gathered.append(copy)

    def forward(at, part):
        copy = remote(out_ref.at[half, part], out_ref.at[half, part], at, {"sub": 1 - half})
        copy.start()
        crossed.append(copy)

    forward(2 * count, me)
    for d, copy in enumerate(gathered):
        copy.wait_recv()
        forward(2 * count + 1 + d, lax.rem(me + count - 1 - d, count))
    for copy in scattered + gathered:
        copy.wait_send()
    for copy in crossed:
        copy.wait()


def tile_sum(x, paired, ident):
    count = lax.axis_size("tile")
    wide = x.size // (2 * count * 16)
    if wide < COLS or lax.axis_size("sub") != 2:
        return lax.psum(x, ("tile", "sub") if paired else "tile")
    block = (count, 16, wide)
    scratch = [
        pltpu.VMEM((count - 1, 16, wide), BF16),
        pltpu.VMEM(block, BF16),
        pltpu.SemaphoreType.DMA((3 * count + 1,)),
        pltpu.SemaphoreType.DMA((3 * count + 1,)),
    ]
    if paired:
        scratch.append(pltpu.VMEM(block, F32))
    out = pl.pallas_call(
        functools.partial(tile_sum_body, count, paired),
        out_shape=jax.ShapeDtypeStruct((2,) + block, BF16),
        in_specs=[pl.BlockSpec(memory_space=pltpu.VMEM)],
        out_specs=pl.BlockSpec(memory_space=pltpu.VMEM),
        scratch_shapes=scratch,
        compiler_params=pltpu.CompilerParams(
            collective_id=ident, has_side_effects=True, vmem_limit_bytes=VMEM_LIMIT
        ),
    )(x.reshape((2,) + block))
    return out.reshape(x.shape)


def prepare_body(slots, steps, here_ref, plan_ref, owner_ref, store_ref, out_ref, held, sems):
    copies = []
    for at, s in enumerate(steps):
        holder = owner_ref[plan_ref[s]]
        copy = pltpu.make_async_copy(store_ref.at[lax.rem(holder, slots)], held.at[at], sems.at[at])
        copy.start()
        copies.append((holder, copy))
    for at, (holder, copy) in enumerate(copies):
        copy.wait()
        mine = lax.div(holder, slots) == here_ref[0]

        @pl.when(mine)
        def _():
            out_ref[at] = held[at].astype(BF16)

        @pl.when(jnp.logical_not(mine))
        def _():
            out_ref[at] = jnp.zeros(out_ref.shape[1:], BF16)


def prepare(store, steps, plan, owner, here):
    slots, count = store.shape[:2]
    smem = pl.BlockSpec(memory_space=pltpu.SMEM)
    return pl.pallas_call(
        functools.partial(prepare_body, slots, steps),
        out_shape=jax.ShapeDtypeStruct((len(steps), count, FEAT), BF16),
        in_specs=[smem, smem, smem, pl.BlockSpec(memory_space=pl.ANY)],
        out_specs=pl.BlockSpec(memory_space=pltpu.VMEM),
        scratch_shapes=[pltpu.VMEM((len(steps), count, FEAT), F32), pltpu.SemaphoreType.DMA((len(steps),))],
        compiler_params=pltpu.CompilerParams(vmem_limit_bytes=VMEM_LIMIT),
    )(here.reshape(1), plan, owner, store)


def permutation():
    side = FEAT // 2
    rows = lax.broadcasted_iota(jnp.int32, (side, side), 0)
    cols = lax.broadcasted_iota(jnp.int32, (side, side), 1)
    source = (cols & 7) * 128 + (cols >> 7) * 16 + ((cols >> 3) & 15)
    return jnp.where(rows == source, 1.0, 0.0).astype(BF16)


def arrange_body(x_ref, out_ref):
    steps, count = x_ref.shape[:2]
    parts = []
    for s in range(steps):
        for high in range(2):
            pieces = [x_ref[s, :, c * 256 + high * 128 : c * 256 + high * 128 + 128] for c in range(C)]
            parts.append(jnp.concatenate(pieces, axis=1))
    moved = jnp.dot(jnp.concatenate(parts, axis=0), permutation(), preferred_element_type=F32).astype(BF16)
    for s in range(steps):
        for high in range(2):
            top = (2 * s + high) * count
            for r in range(8):
                m = PATCH - 1 - (high * 8 + r)
                out_ref[s, :, m * QC : (m + 1) * QC] = moved[top : top + count, r * QC : (r + 1) * QC]


def restore_body(x_ref, out_ref):
    steps, count = x_ref.shape[:2]
    side = FEAT // 2
    parts = [x_ref[s, :, high * side : (high + 1) * side] for s in range(steps) for high in range(2)]
    moved = lax.dot_general(
        jnp.concatenate(parts, axis=0).astype(BF16),
        permutation(),
        (((1,), (1,)), ((), ())),
        preferred_element_type=F32,
    )
    for s in range(steps):
        for high in range(2):
            top = (2 * s + high) * count
            for c in range(C):
                out_ref[s, :, c * 256 + high * 128 : c * 256 + high * 128 + 128] = moved[
                    top : top + count, c * 128 : c * 128 + 128
                ]


def swap_halo(x, place):
    send = jnp.where(place == 0, x[ROWS - HALO :], x[:HALO])
    got = lax.ppermute(send, "sub", [(0, 1), (1, 0)])
    empty = jnp.zeros_like(got)
    return jnp.where(place == 1, got, empty), jnp.where(place == 0, got, empty)


def per_device(residual, coefficients, filter_store, plan, owner):
    scaling = FEAT ** (-0.5)
    sub_place = lax.axis_index("sub")
    tile_place = lax.axis_index("tile")
    pixel_total = float(lax.axis_size("tile") * lax.axis_size("sub") * ROWS * COLS)
    slot_count, count = filter_store.shape[:2]
    holders = [owner[plan[s]] for s in range(STEPS)]
    macs = 2 * count * FEAT * ROWS * COLS

    def picked(store, s):
        return lax.dynamic_index_in_dim(store, holders[s] % slot_count, 0, keepdims=False)

    def shared(store, steps, ident):
        sent = prepare(store, steps, plan, owner, tile_place)
        wholes = [tile_sum(sent[:1], False, ident)] + [lax.psum(sent[at : at + 1], "tile") for at in range(1, len(steps))]
        return [call(arrange_body, jax.ShapeDtypeStruct(w.shape, BF16), [], macs, (w,)) for w in wholes]

    def updated(store, s, grads):
        master = picked(store, s)
        moved = master - FILTER_STEP * grads / pixel_total
        length = jnp.sqrt(jnp.sum(moved * moved, axis=1, keepdims=True)) * scaling
        final = moved / jnp.maximum(length, 1.0)
        written = lax.dynamic_update_index_in_dim(store, final, holders[s] % slot_count, 0)
        return jnp.where(tile_place == holders[s] // slot_count, written, store)

    def summed(local, ident):
        whole = tile_sum(jnp.stack(local), True, ident)
        return call(restore_body, jax.ShapeDtypeStruct(whole.shape, F32), [], macs, (whole,))

    current = residual[0].transpose(1, 0, 2)
    first_pair = shared(filter_store, (0, 1), 0)
    weights = first_pair[0][0]
    fresh_maps, local_grads = [], []
    same = plan[0] == plan[1]
    for s in range(STEPS):
        previous = lax.dynamic_index_in_dim(coefficients[0], plan[s], 0, keepdims=False).transpose(1, 0, 2)
        if s == 1:
            previous = jnp.where(same, fresh_maps[0], previous)
            weights = lax.cond(
                same,
                lambda local, later: shared(updated(filter_store, 0, summed([local], 2)[0]), (1,), 3)[0][0],
                lambda local, later: later[0],
                local_grads[0],
                first_pair[1],
            )
        rounded = current.astype(BF16)
        before, after = swap_halo(rounded, sub_place)
        padded = jnp.concatenate([before, rounded, after], axis=0).astype(F32)
        maps = jax.ShapeDtypeStruct((ROWS, count, COLS), BF16)
        fresh, change = call(
            functools.partial(adjoint_body, count),
            (maps, maps),
            [pltpu.VMEM((PADDED * QC, COLS), BF16)],
            macs,
            (padded, weights, previous),
        )
        edges = swap_halo(jnp.stack([change, fresh], axis=1), sub_place)
        flat = lambda x: x.reshape(-1, COLS)
        space = pltpu.VMEM((PADDED * count, COLS), BF16)
        partial_sum = call(
            functools.partial(synthesis_body, count),
            jax.ShapeDtypeStruct((ROWS, C, COLS), BF16),
            [space, pltpu.VMEM((QC, PATCH * count), BF16)],
            macs,
            (weights, flat(edges[0][:, 0]), flat(change), flat(edges[1][:, 0])),
        )
        if lax.axis_size("chan") == 2:
            other = lax.ppermute(partial_sum, "chan", [(0, 1), (1, 0)])
            total = partial_sum.astype(F32) + other.astype(F32)
        else:
            total = lax.psum(partial_sum, "chan").astype(F32)
        current = current + scaling * total
        target = current.astype(BF16).astype(F32)
        local = call(
            functools.partial(gradient_body, count),
            jax.ShapeDtypeStruct((count, FEAT), F32),
            [space, pltpu.VMEM((PATCH * count, QC), F32)],
            macs,
            (target, flat(edges[0][:, 1]), flat(fresh), flat(edges[1][:, 1])),
        )
        fresh_maps.append(fresh)
        local_grads.append(local)
    sums = summed(local_grads, 1)
    store = filter_store
    for s in range(STEPS):
        store = updated(store, s, sums[s])
    coeffs_out = jnp.stack(fresh_maps, axis=0).transpose(0, 2, 1, 3)
    return (current.transpose(1, 0, 2)[None], coeffs_out[None], store)


def solution(mesh):
    placed = (
        P(("groups", "tile"), None, "sub", None),
        P(("groups", "tile"), None, "chan", "sub", None),
        P(("groups", "tile"), "chan", None),
        P(),
        P(),
    )
    return jax.shard_map(
        per_device,
        mesh=mesh,
        in_specs=placed,
        out_specs=(
            P(("groups", "tile"), None, "sub", None),
            P(("groups", "tile"), None, "chan", "sub", None),
            P(("groups", "tile"), "chan", None),
        ),
        check_vma=False,
    )
```
